32 devices in a mesh: row: 8 (over z, y), col: 4 (over x, core).
Axes of the slice: x: 2, y: 2, z: 4, core: 2. Of those that a mesh axis runs over, the one named last changes fastest.
Arguments:
- trailing: float32 [8192, 4096], P('row', 'col'), may hold values from -6 to 6
- panel_y: float32 [8192, 256], P(('row', 'col')), may hold values from -0.1875 to 0.1875
- panel_t: float32 [2048, 256], P('row'), may hold values from 0.5 to 1.5
- tree_v: float32 [3, 2048, 256], P(None, 'row'), may hold values from -0.375 to 0.375, as said below
- tree_t: float32 [3, 2048, 256], P(None, 'row'), may hold values from 0.5 to 1.5, as said below
Outputs:
- updated: float32 [8192, 4096], P('row', 'col')
The draws below stay inside these ranges and needn't reach their ends.
Inputs may be any that keep to these rules, and one draw needn't show every extreme that they name: For each level l, the blocks of 256 rows that tree_v[l] holds for two tile rows that differ only in bit l are equal. For each level l, the blocks of 256 rows that tree_t[l] holds for two tile rows that differ only in bit l are equal.
All inputs are finite; a program needn't handle non-finite values.
Results may differ from the reference program's by a relative error of at most 0.0001.
Values sent between devices are 32-bit elements; how exact they have to be, the bound alone decides.
A program may use at most 64 MiB of HBM per device.

```python
import math
import jax
import jax.numpy as jnp
from jax import lax

B = 256
M_DEV = 1024
LEVELS = 3
M = 8192
N = 4096
N_ROW = 8


def pair_copy(base):
    levels = []
    for level in range(LEVELS):
        leads = jnp.arange(N_ROW) & ~(1 << level)
        levels.append(base[level][leads])
    return jnp.stack(levels).reshape(LEVELS, N_ROW * B, B)


def draw_tree_v(key, part):
    base = jax.random.normal(key, (LEVELS, N_ROW, B, B), jnp.float32) * (1.0 / math.sqrt(B))
    base = jnp.clip(base, -0.375, 0.375)
    return pair_copy(base)


def draw_tree_t(key, part):
    base = jax.random.uniform(key, (LEVELS, N_ROW, B, B), jnp.float32, 0.5, 1.5)
    return pair_copy(base)


def level_of(key, extent, cuts, low, largest):
    gain, own = 1.0, jax.random.fold_in(key, 6)
    for position, shards_of in cuts:
        heights = jnp.exp(jax.random.uniform(jax.random.fold_in(own, position), (shards_of,), jnp.float32, low / len(cuts), largest / len(cuts)))
        gain = gain * jnp.repeat(heights, extent[position] // shards_of).reshape([-1 if axis == position else 1 for axis in range(len(extent))])
    return gain


def centred(stream_key, dims, scale, reach, shards=(), kind=jnp.bfloat16):
    drawn = scale * jax.random.normal(stream_key, dims, jnp.float32)
    if shards:
        drawn = drawn * level_of(stream_key, dims, shards, -0.22, 0.18)
    return jnp.clip(drawn, -reach, reach).astype(kind)


def setup_inputs(seed: int = 0) -> dict:
    arg_keys = jax.random.split(jax.random.key(seed), 6)
    return {
        "trailing": centred(arg_keys[0], (M, N), 1.0, 6.0, ((0, 8), (1, 4)), jnp.float32),
        "panel_y": centred(arg_keys[1], (M, B), M_DEV ** -0.5, 0.1875, ((0, 32),), jnp.float32),
        "panel_t": jnp.clip(0.5 + 1.0 * jax.random.uniform(arg_keys[2], (N_ROW * B, B), jnp.float32) ** level_of(arg_keys[2], (N_ROW * B, B), ((0, 8),), -0.2, 0.2), 0.5, 1.5),
        "tree_v": draw_tree_v(jax.random.fold_in(arg_keys[5], 71), 0),
        "tree_t": draw_tree_t(jax.random.fold_in(arg_keys[5], 71), 0),
    }


def unit_lower(values):
    rows = jnp.arange(values.shape[-2])[:, None]
    cols = jnp.arange(values.shape[-1])[None, :]
    return jnp.where(rows > cols, values, jnp.where(rows == cols, jnp.float32(1.0), jnp.float32(0.0)))

def triangle_factor(values):
    width = values.shape[-1]
    rows = jnp.arange(width)[:, None]
    cols = jnp.arange(width)[None, :]
    scale = 2.0 / math.sqrt(width)
    return jnp.where(rows == cols, values, jnp.where(cols > rows, (values - 1.0) * scale, jnp.float32(0.0)))

def upper_part(values):
    width = values.shape[-1]
    rows = jnp.arange(width)[:, None]
    cols = jnp.arange(width)[None, :]
    return jnp.where(cols >= rows, values, jnp.float32(0.0))

def reference(trailing, panel_y, panel_t, tree_v, tree_t):
    highest = lax.Precision.HIGHEST
    blocks = trailing.reshape(N_ROW, M_DEV, N)
    reflect = panel_y.reshape(N_ROW, M_DEV, B)
    factors = panel_t.reshape(N_ROW, B, B)

    def local_update(pieces):
        block, vectors, tri = pieces
        lower = unit_lower(vectors)
        proj = jnp.einsum('mb,mn->bn', lower, block, precision=highest)
        weight = jnp.einsum('kb,kn->bn', triangle_factor(tri), proj, precision=highest)
        return block - jnp.einsum('mb,bn->mn', lower, weight, precision=highest)
    local = lax.map(local_update, (blocks, reflect, factors))
    tops = local[:, :B, :]
    for level in range(LEVELS):
        span = 1 << level
        groups = N_ROW // (2 * span)
        paired = tops.reshape(groups, 2, span, B, N)
        first = paired[:, 0]
        second = paired[:, 1]
        vees = upper_part(tree_v[level].reshape(groups, 2, span, B, B)[:, 0])
        tees = triangle_factor(tree_t[level].reshape(groups, 2, span, B, B)[:, 0])
        summed = first + jnp.einsum('gskb,gskn->gsbn', vees, second, precision=highest)
        weight = jnp.einsum('gskb,gskn->gsbn', tees, summed, precision=highest)
        new_first = first - weight
        new_second = second - jnp.einsum('gsbk,gskn->gsbn', vees, weight, precision=highest)
        tops = jnp.stack([new_first, new_second], axis=1).reshape(N_ROW, B, N)
    local = local.at[:, :B, :].set(tops)
    return local.reshape(M, N)
```

```python
import functools
import math

import jax
import jax.numpy as jnp
from jax import lax
from jax.experimental import pallas as pl
from jax.experimental.pallas import tpu as pltpu
from jax.sharding import PartitionSpec as P

CHUNK = 128
MESH = pl.DeviceIdType.MESH


def split(x):
    high = x.astype(jnp.bfloat16)
    low = (x - high.astype(jnp.float32)).astype(jnp.bfloat16)
    return high, low


def dot3(lhs_high, lhs_low, rhs):
    high, low = split(rhs)
    dot = functools.partial(jnp.dot, preferred_element_type=jnp.float32)
    return dot(lhs_high, high) + (dot(lhs_high, low) + dot(lhs_low, high))


def grid_of(shape, row_offset=0):
    rows = lax.broadcasted_iota(jnp.int32, shape, 0) + row_offset
    cols = lax.broadcasted_iota(jnp.int32, shape, 1)
    return rows, cols


def triangle_factor(values):
    width = values.shape[-1]
    rows, cols = grid_of(values.shape)
    scale = 2.0 / math.sqrt(width)
    return jnp.where(
        rows == cols, values, jnp.where(cols > rows, (values - 1.0) * scale, jnp.float32(0.0))
    )


def kernel(
    n_col, levels, chunks, width, depth,
    c_hbm, y_hbm, t_hbm, v_hbm, tt_hbm, out_hbm,
    c_v, y_v, t_v, v_v, tt_v, w_v, z_v, r_v,
    yt_s, yb_s, t_s, at_s, b_s,
    c_sem, in_sem, out_sem, ys_sem, yr_sem, s_sem, r_sem,
):
    row = lax.axis_index("row")
    col = lax.axis_index("col")
    chunk = c_v.shape[2]
    rest = c_v.shape[1] - width
    bits = [1 << b for b in range(n_col.bit_length() - 2, -1, -1)]

    def columns(k):
        return pl.ds(pl.multiple_of(k * chunk, chunk), chunk)

    def load_c(k):
        return pltpu.make_async_copy(c_hbm.at[:, columns(k)], c_v.at[k], c_sem.at[k])

    own_y = pltpu.make_async_copy(y_hbm, y_v.at[col], in_sem.at[0])
    load_t = pltpu.make_async_copy(t_hbm, t_v, in_sem.at[1])
    load_v = pltpu.make_async_copy(v_hbm, v_v, in_sem.at[2])
    load_tt = pltpu.make_async_copy(tt_hbm, tt_v, in_sem.at[3])
    own_y.start()

    barrier = pltpu.get_barrier_semaphore()
    partners = [(row, col ^ bit) for bit in bits]
    partners += [(row ^ (1 << level), col) for level in range(levels)]
    for partner in partners:
        pl.semaphore_signal(barrier, inc=1, device_id=partner, device_id_type=MESH)
    load_v.start()
    load_tt.start()
    load_t.start()
    for k in range(chunks):
        load_c(k).start()
    own_y.wait()
    pl.semaphore_wait(barrier, len(partners))

    def send_y(off, bit):
        block = col ^ off
        return pltpu.make_async_remote_copy(
            src_ref=y_v.at[block],
            dst_ref=y_v.at[block],
            send_sem=ys_sem.at[off | bit],
            recv_sem=yr_sem.at[off | bit],
            device_id=(row, col ^ bit),
            device_id_type=MESH,
        )

    def arrived_y(off):
        return pltpu.make_async_remote_copy(
            src_ref=y_v.at[col ^ off],
            dst_ref=y_v.at[col ^ off],
            send_sem=ys_sem.at[off],
            recv_sem=yr_sem.at[off],
            device_id=(row, col ^ 1),
            device_id_type=MESH,
        )

    for bit in bits:
        send_y(0, bit).start()

    load_v.wait()
    load_tt.wait()
    load_t.wait()
    high, low = split(triangle_factor(t_v[...]).T)
    t_s[0], t_s[1] = high, low
    for level in range(levels):
        leader = (row >> level) & 1 == 0
        rows, cols = grid_of((width, width))
        vees = jnp.where(cols >= rows, v_v[level], jnp.float32(0.0))
        at_s[level, 0], at_s[level, 1] = split(vees.T)
        tees = triangle_factor(tt_v[level]).T
        vees_high, vees_low = split(vees)
        both = jnp.where(leader, tees, dot3(vees_high, vees_low, tees))
        b_s[level, 0], b_s[level, 1] = split(both)

    def take_y(off):
        block = col ^ off
        rows, cols = grid_of((depth, width), block * depth)
        lower = jnp.where(
            rows > cols,
            y_v[block],
            jnp.where(rows == cols, jnp.float32(1.0), jnp.float32(0.0)),
        )
        place = pl.ds(pl.multiple_of(block * depth, depth), depth)
        high, low = split(lower)
        yb_s[0, place, :] = high
        yb_s[1, place, :] = low
        high, low = split(lower.T)
        yt_s[0, :, place] = high
        yt_s[1, :, place] = low

    take_y(0)
    order = sorted(range(1, n_col), key=lambda off: (bin(off).count("1"), off))
    for off in order:
        arrived_y(off).wait_recv()
        for bit in bits:
            if bit < off & -off:
                send_y(off, bit).start()
        take_y(off)

    def exchange(level, k):
        return pltpu.make_async_remote_copy(
            src_ref=z_v.at[level, k],
            dst_ref=r_v.at[level, k],
            send_sem=s_sem.at[level, k],
            recv_sem=r_sem.at[level, k],
            device_id=(row ^ (1 << level), col),
            device_id_type=MESH,
        )

    def give(level, k, top):
        leader = (row >> level) & 1 == 0
        down = dot3(at_s[level, 0], at_s[level, 1], top)
        z_v[level, k] = jnp.where(leader, top, down)
        exchange(level, k).start()

    def local(k):
        load_c(k).wait()
        proj = dot3(yt_s[0], yt_s[1], c_v[k])
        weight = dot3(t_s[0], t_s[1], proj)
        w_v[k] = weight
        top = c_v[k, :width, :] - dot3(yb_s[0, :width, :], yb_s[1, :width, :], weight)
        c_v[k, :width, :] = top
        give(0, k, top)

    def combine(level, k):
        exchange(level, k).wait_recv()
        total = z_v[level, k] + r_v[level, k]
        top = c_v[k, :width, :] - dot3(b_s[level, 0], b_s[level, 1], total)
        c_v[k, :width, :] = top
        return top

    def store_top(k):
        return pltpu.make_async_copy(
            c_v.at[k, pl.ds(0, width), :], out_hbm.at[pl.ds(0, width), columns(k)], out_sem.at[0, k]
        )

    def store_rest(k):
        return pltpu.make_async_copy(
            c_v.at[k, pl.ds(width, rest), :],
            out_hbm.at[pl.ds(width, rest), columns(k)],
            out_sem.at[1, k],
        )

    def step(t, carry):
        @pl.when(t < chunks)
        def _():
            local(t)

        for level in range(levels - 1):
            k = t - 1 - level

            @pl.when((k >= 0) & (k < chunks))
            def _():
                top = combine(level, k)
                give(level + 1, k, top)

        return carry

    lax.fori_loop(0, chunks + levels - 1, step, 0)

    def finish(k, carry):
        c_v[k, width:, :] = c_v[k, width:, :] - dot3(
            yb_s[0, width:, :], yb_s[1, width:, :], w_v[k]
        )
        store_rest(k).start()
        combine(levels - 1, k)
        store_top(k).start()
        return carry

    lax.fori_loop(0, chunks, finish, 0)

    for bit in bits:
        for off in range(0, n_col, 2 * bit):
            send_y(off, bit).wait_send()

    def drain(k, carry):
        for level in range(levels):
            exchange(level, k).wait_send()
        store_top(k).wait()
        store_rest(k).wait()
        return carry

    lax.fori_loop(0, chunks, drain, 0)


def per_device(trailing, panel_y, panel_t, tree_v, tree_t):
    n_col = lax.axis_size("col")
    depth, width = panel_y.shape
    height, extent = trailing.shape
    levels = tree_v.shape[0]
    chunk = min(CHUNK, extent)
    chunks = extent // chunk
    f32, bf16 = jnp.float32, jnp.bfloat16
    products = height * width * 2 + width * width * (1 + 2 * levels)
    return pl.pallas_call(
        functools.partial(kernel, n_col, levels, chunks, width, depth),
        out_shape=jax.ShapeDtypeStruct(trailing.shape, f32),
        in_specs=[pl.BlockSpec(memory_space=pltpu.HBM)] * 5,
        out_specs=pl.BlockSpec(memory_space=pl.ANY),
        scratch_shapes=[
            pltpu.VMEM((chunks, height, chunk), f32),
            pltpu.VMEM((n_col, depth, width), f32),
            pltpu.VMEM((width, width), f32),
            pltpu.VMEM((levels, width, width), f32),
            pltpu.VMEM((levels, width, width), f32),
            pltpu.VMEM((chunks, width, chunk), f32),
            pltpu.VMEM((levels, chunks, width, chunk), f32),
            pltpu.VMEM((levels, chunks, width, chunk), f32),
            pltpu.VMEM((2, width, height), bf16),
            pltpu.VMEM((2, height, width), bf16),
            pltpu.VMEM((2, width, width), bf16),
            pltpu.VMEM((levels, 2, width, width), bf16),
            pltpu.VMEM((levels, 2, width, width), bf16),
            pltpu.SemaphoreType.DMA((chunks,)),
            pltpu.SemaphoreType.DMA((4,)),
            pltpu.SemaphoreType.DMA((2, chunks)),
            pltpu.SemaphoreType.DMA((n_col,)),
            pltpu.SemaphoreType.DMA((n_col,)),
            pltpu.SemaphoreType.DMA((levels, chunks)),
            pltpu.SemaphoreType.DMA((levels, chunks)),
        ],
        compiler_params=pltpu.CompilerParams(
            collective_id=0, has_side_effects=True, vmem_limit_bytes=40 * 1024 * 1024
        ),
        cost_estimate=pl.CostEstimate(
            flops=6 * products * extent,
            bytes_accessed=8 * height * extent,
            transcendentals=0,
        ),
    )(trailing, panel_y, panel_t, tree_v, tree_t)


def solution(mesh):
    placed = (
        P("row", "col"),
        P(("row", "col"), None),
        P("row", None),
        P(None, "row", None),
        P(None, "row", None),
    )
    return jax.shard_map(
        per_device, mesh=mesh, in_specs=placed, out_specs=P("row", "col"), check_vma=False
    )
```

```python
import functools
import math

import jax
import jax.numpy as jnp
from jax import lax
from jax.experimental import pallas as pl
from jax.experimental.pallas import tpu as pltpu
from jax.sharding import PartitionSpec as P

CHUNK = 128
PARTS = 2
MESH = pl.DeviceIdType.MESH


def split(x):
    high = x.astype(jnp.bfloat16)
    low = (x - high.astype(jnp.float32)).astype(jnp.bfloat16)
    return high, low


def stack(x):
    return jnp.concatenate(split(x), axis=0)


def dot3(lhs, rhs):
    half = lhs.shape[0] // 2
    high, low = split(rhs)
    both = jnp.dot(lhs, high, preferred_element_type=jnp.float32)
    cross = jnp.dot(lhs[:half], low, preferred_element_type=jnp.float32)
    return both[:half] + (both[half:] + cross)


def grid_of(shape, row_offset=0):
    rows = lax.broadcasted_iota(jnp.int32, shape, 0) + row_offset
    cols = lax.broadcasted_iota(jnp.int32, shape, 1)
    return rows, cols


def triangle_factor(values):
    width = values.shape[-1]
    rows, cols = grid_of(values.shape)
    scale = 2.0 / math.sqrt(width)
    return jnp.where(
        rows == cols, values, jnp.where(cols > rows, (values - 1.0) * scale, jnp.float32(0.0))
    )


def kernel(
    n_col, levels, chunks, width, depth, parts,
    c_hbm, y_hbm, t_hbm, v_hbm, tt_hbm, out_hbm,
    c_v, y_v, t_v, v_v, tt_v, p_v, w_v, z_v, r_v,
    yr_s, t_s, a_s, b_s, f_s,
    c_sem, in_sem, out_sem, ys_sem, yr_sem, s_sem, r_sem,
):
    row = lax.axis_index("row")
    col = lax.axis_index("col")
    chunk = c_v.shape[2]
    rest = c_v.shape[1] - width
    pairs = chunks // 2
    share = depth // parts
    bits = [1 << b for b in range(n_col.bit_length() - 2, -1, -1)]

    def columns(k):
        return pl.ds(pl.multiple_of(k * chunk, chunk), chunk)

    def load_c(k):
        return pltpu.make_async_copy(c_hbm.at[:, columns(k)], c_v.at[k], c_sem.at[k])

    own_y = pltpu.make_async_copy(y_hbm, y_v.at[col], in_sem.at[0])
    load_t = pltpu.make_async_copy(t_hbm, t_v, in_sem.at[1])
    load_v = pltpu.make_async_copy(v_hbm, v_v, in_sem.at[2])
    load_tt = pltpu.make_async_copy(tt_hbm, tt_v, in_sem.at[3])
    own_y.start()

    barrier = pltpu.get_barrier_semaphore()
    partners = [(row, col ^ bit) for bit in bits]
    partners += [(row ^ (1 << level), col) for level in range(levels)]
    for partner in partners:
        pl.semaphore_signal(barrier, inc=1, device_id=partner, device_id_type=MESH)
    load_v.start()
    load_tt.start()
    load_t.start()
    for k in range(chunks):
        load_c(k).start()
    own_y.wait()
    pl.semaphore_wait(barrier, len(partners))

    def send_y(off, bit, part):
        place = y_v.at[col ^ off, pl.ds(part * share, share), :]
        return pltpu.make_async_remote_copy(
            src_ref=place,
            dst_ref=place,
            send_sem=ys_sem.at[part, off | bit],
            recv_sem=yr_sem.at[part, off | bit],
            device_id=(row, col ^ bit),
            device_id_type=MESH,
        )

    def arrived_y(off, part):
        place = y_v.at[col ^ off, pl.ds(part * share, share), :]
        return pltpu.make_async_remote_copy(
            src_ref=place,
            dst_ref=place,
            send_sem=ys_sem.at[part, off],
            recv_sem=yr_sem.at[part, off],
            device_id=(row, col ^ 1),
            device_id_type=MESH,
        )

    for bit in bits:
        for part in range(parts):
            send_y(0, bit, part).start()

    def pair_of(p, rows):
        return jnp.concatenate([c_v[2 * p, rows, :], c_v[2 * p + 1, rows, :]], axis=1)

    def leads(level):
        return (row >> level) & 1 == 0

    def prepare(level):
        rows, cols = grid_of((width, width))
        vees = jnp.where(cols >= rows, v_v[level], jnp.float32(0.0))
        a_s[level] = stack(vees.T)
        tees = triangle_factor(tt_v[level]).T
        both = jnp.where(leads(level), tees, dot3(stack(vees), tees))
        terms = split(both)
        if level == levels - 1:
            b_s[level, :width], b_s[level, 2 * width : 3 * width] = terms
        else:
            rows, cols = grid_of((width, width))
            after = jnp.where(cols >= rows, v_v[level + 1], jnp.float32(0.0)).T
            folded = split(jnp.where(leads(level + 1), both, dot3(stack(after), both)))
            for i in range(2):
                b_s[level, 2 * i * width : (2 * i + 1) * width] = terms[i]
                b_s[level, (2 * i + 1) * width : (2 * i + 2) * width] = folded[i]

    def take_y(off):
        block = col ^ off
        rows, cols = grid_of((depth, width), block * depth)
        lower = jnp.where(
            rows > cols,
            y_v[block],
            jnp.where(rows == cols, jnp.float32(1.0), jnp.float32(0.0)),
        )
        place = pl.ds(pl.multiple_of(block * depth, depth), depth)
        high, low = split(lower)
        yr_s[0, place, :] = high
        yr_s[1, place, :] = low
        across = stack(lower.T)
        for p in range(pairs):
            term = dot3(across, pair_of(p, place))
            p_v[p] = term if off == 0 else p_v[p] + term

    load_v.wait()
    load_tt.wait()
    load_t.wait()
    t_s[...] = stack(triangle_factor(t_v[...]).T)
    prepare(0)
    for k in range(chunks):
        load_c(k).wait()
    for p in range(pairs):
        top = pair_of(p, slice(0, width))
        ahead = jnp.where(leads(0), top, dot3(a_s[0], top))
        z_v[0, 2 * p] = ahead[:, :chunk]
        z_v[0, 2 * p + 1] = ahead[:, chunk:]
    take_y(0)
    order = sorted(range(1, n_col), key=lambda off: (bin(off).count("1"), off))
    for off in order:
        for part in range(parts):
            arrived_y(off, part).wait_recv()
            for bit in bits:
                if bit < off & -off:
                    send_y(off, bit, part).start()
        if off == order[0]:
            take_y(off)
            for level in range(1, levels):
                prepare(level)
        else:
            take_y(off)
    upper = jnp.concatenate([yr_s[0, :width, :], yr_s[1, :width, :]], axis=0)
    straight = upper[:width].astype(jnp.float32) + upper[width:].astype(jnp.float32)
    folded = split(jnp.where(leads(0), straight, dot3(a_s[0], straight)))
    for i in range(2):
        f_s[2 * i * width : (2 * i + 1) * width] = yr_s[i, :width, :]
        f_s[(2 * i + 1) * width : (2 * i + 2) * width] = folded[i]

    def exchange(level, k):
        return pltpu.make_async_remote_copy(
            src_ref=z_v.at[level, k],
            dst_ref=r_v.at[level, k],
            send_sem=s_sem.at[level, k],
            recv_sem=r_sem.at[level, k],
            device_id=(row ^ (1 << level), col),
            device_id_type=MESH,
        )

    def local(p):
        weight = dot3(t_s[...], p_v[p])
        w_v[p] = weight
        change = dot3(f_s[...], weight)
        for i in range(2):
            k = 2 * p + i
            side = slice(i * chunk, (i + 1) * chunk)
            z_v[0, k] = z_v[0, k] - change[width:, side]
            exchange(0, k).start()
            c_v[k, :width, :] = c_v[k, :width, :] - change[:width, side]

    def combine(level, k):
        top = c_v[k, :width, :]
        ahead = jnp.where(leads(level + 1), top, dot3(a_s[level + 1], top))
        exchange(level, k).wait_recv()
        change = dot3(b_s[level], z_v[level, k] + r_v[level, k])
        z_v[level + 1, k] = ahead - change[width:]
        exchange(level + 1, k).start()
        c_v[k, :width, :] = top - change[:width]

    def last(k):
        level = levels - 1
        exchange(level, k).wait_recv()
        lhs = jnp.concatenate([b_s[level, :width], b_s[level, 2 * width : 3 * width]], axis=0)
        c_v[k, :width, :] = c_v[k, :width, :] - dot3(lhs, z_v[level, k] + r_v[level, k])

    def store_top(k):
        return pltpu.make_async_copy(
            c_v.at[k, pl.ds(0, width), :], out_hbm.at[pl.ds(0, width), columns(k)], out_sem.at[0, k]
        )

    def store_rest(k):
        return pltpu.make_async_copy(
            c_v.at[k, pl.ds(width, rest), :],
            out_hbm.at[pl.ds(width, rest), columns(k)],
            out_sem.at[1, k],
        )

    local(0)

    def step(t, carry):
        @pl.when((lax.rem(t, 2) == 0) & (t // 2 + 1 < pairs))
        def _():
            local(t // 2 + 1)

        for level in range(levels - 1):
            k = t - level

            @pl.when((k >= 0) & (k < chunks))
            def _():
                combine(level, k)

        return carry

    lax.fori_loop(0, chunks + levels - 2, step, 0)

    def finish(p, carry):
        lhs = jnp.concatenate([yr_s[0, width:, :], yr_s[1, width:, :]], axis=0)
        change = dot3(lhs, w_v[p])
        for i in range(2):
            k = 2 * p + i
            c_v[k, width:, :] = c_v[k, width:, :] - change[:, i * chunk : (i + 1) * chunk]
            store_rest(k).start()
        for i in range(2):
            last(2 * p + i)
            store_top(2 * p + i).start()
        return carry

    lax.fori_loop(0, pairs, finish, 0)

    for bit in bits:
        for off in range(0, n_col, 2 * bit):
            for part in range(parts):
                send_y(off, bit, part).wait_send()

    def drain(k, carry):
        for level in range(levels):
            exchange(level, k).wait_send()
        store_top(k).wait()
        store_rest(k).wait()
        return carry

    lax.fori_loop(0, chunks, drain, 0)


def per_device(trailing, panel_y, panel_t, tree_v, tree_t):
    n_col = lax.axis_size("col")
    depth, width = panel_y.shape
    height, extent = trailing.shape
    levels = tree_v.shape[0]
    chunk = min(CHUNK, extent)
    chunks = extent // chunk
    f32, bf16 = jnp.float32, jnp.bfloat16
    products = height * width * 2 + width * width * (1 + 2 * levels)
    return pl.pallas_call(
        functools.partial(kernel, n_col, levels, chunks, width, depth, PARTS),
        out_shape=pltpu.VMEM(trailing.shape, f32),
        in_specs=[pl.BlockSpec(memory_space=pltpu.HBM)] * 5,
        out_specs=pl.BlockSpec(memory_space=pl.ANY),
        scratch_shapes=[
            pltpu.VMEM((chunks, height, chunk), f32),
            pltpu.VMEM((n_col, depth, width), f32),
            pltpu.VMEM((width, width), f32),
            pltpu.VMEM((levels, width, width), f32),
            pltpu.VMEM((levels, width, width), f32),
            pltpu.VMEM((chunks // 2, width, 2 * chunk), f32),
            pltpu.VMEM((chunks // 2, width, 2 * chunk), f32),
            pltpu.VMEM((levels, chunks, width, chunk), f32),
            pltpu.VMEM((levels, chunks, width, chunk), f32),
            pltpu.VMEM((2, height, width), bf16),
            pltpu.VMEM((2 * width, width), bf16),
            pltpu.VMEM((levels, 2 * width, width), bf16),
            pltpu.VMEM((levels, 4 * width, width), bf16),
            pltpu.VMEM((4 * width, width), bf16),
            pltpu.SemaphoreType.DMA((chunks,)),
            pltpu.SemaphoreType.DMA((4,)),
            pltpu.SemaphoreType.DMA((2, chunks)),
            pltpu.SemaphoreType.DMA((PARTS, n_col)),
            pltpu.SemaphoreType.DMA((PARTS, n_col)),
            pltpu.SemaphoreType.DMA((levels, chunks)),
            pltpu.SemaphoreType.DMA((levels, chunks)),
        ],
        compiler_params=pltpu.CompilerParams(
            collective_id=0, has_side_effects=True, vmem_limit_bytes=56 * 1024 * 1024
        ),
        cost_estimate=pl.CostEstimate(
            flops=6 * products * extent,
            bytes_accessed=8 * height * extent,
            transcendentals=0,
        ),
    )(trailing, panel_y, panel_t, tree_v, tree_t)


def solution(mesh):
    placed = (
        P("row", "col"),
        P(("row", "col"), None),
        P("row", None),
        P(None, "row", None),
        P(None, "row", None),
    )
    return jax.shard_map(
        per_device, mesh=mesh, in_specs=placed, out_specs=P("row", "col"), check_vma=False
    )
```

```python
import functools
import math

import jax
import jax.numpy as jnp
from jax import lax
from jax.experimental import pallas as pl
from jax.experimental.pallas import tpu as pltpu
from jax.sharding import PartitionSpec as P

CHUNK = 128
PARTS = 2
MESH = pl.DeviceIdType.MESH


def split(x):
    high = x.astype(jnp.bfloat16)
    low = (x - high.astype(jnp.float32)).astype(jnp.bfloat16)
    return high, low


def stack(x):
    return jnp.concatenate(split(x), axis=0)


def dot3(lhs, rhs):
    half = lhs.shape[0] // 2
    high, low = split(rhs)
    both = jnp.dot(lhs, high, preferred_element_type=jnp.float32)
    cross = jnp.dot(lhs[:half], low, preferred_element_type=jnp.float32)
    return both[:half] + (both[half:] + cross)


def grid_of(shape, row_offset=0):
    rows = lax.broadcasted_iota(jnp.int32, shape, 0) + row_offset
    cols = lax.broadcasted_iota(jnp.int32, shape, 1)
    return rows, cols


def triangle_factor(values):
    width = values.shape[-1]
    rows, cols = grid_of(values.shape)
    scale = 2.0 / math.sqrt(width)
    return jnp.where(
        rows == cols, values, jnp.where(cols > rows, (values - 1.0) * scale, jnp.float32(0.0))
    )


def kernel(
    n_col, levels, chunks, width, depth, parts,
    c_hbm, y_hbm, t_hbm, v_hbm, tt_hbm, out_hbm,
    c_v, y_v, t_v, v_v, tt_v, p_v, w_v, z_v, r_v,
    yr_s, yt_s, t_s, a_s, b_s, f_s,
    c_sem, in_sem, out_sem, ys_sem, yr_sem, s_sem, r_sem,
):
    row = lax.axis_index("row")
    col = lax.axis_index("col")
    chunk = c_v.shape[2]
    rest = c_v.shape[1] - width
    pairs = chunks // 2
    share = depth // parts
    bits = [1 << b for b in range(n_col.bit_length() - 2, -1, -1)]

    def columns(k):
        return pl.ds(pl.multiple_of(k * chunk, chunk), chunk)

    def load_c(k):
        return pltpu.make_async_copy(c_hbm.at[:, columns(k)], c_v.at[k], c_sem.at[k])

    own_y = pltpu.make_async_copy(y_hbm, y_v.at[col], in_sem.at[0])
    load_t = pltpu.make_async_copy(t_hbm, t_v, in_sem.at[1])
    load_v = pltpu.make_async_copy(v_hbm, v_v, in_sem.at[2])
    load_tt = pltpu.make_async_copy(tt_hbm, tt_v, in_sem.at[3])
    own_y.start()

    barrier = pltpu.get_barrier_semaphore()
    partners = [(row, col ^ bit) for bit in bits]
    partners += [(row ^ (1 << level), col) for level in range(levels)]
    for partner in partners:
        pl.semaphore_signal(barrier, inc=1, device_id=partner, device_id_type=MESH)
    load_v.start()
    load_tt.start()
    load_t.start()
    for k in range(chunks):
        load_c(k).start()
    pl.semaphore_wait(barrier, len(partners))

    def send_y(off, bit, part):
        place = y_v.at[col ^ off, pl.ds(part * share, share), :]
        return pltpu.make_async_remote_copy(
            src_ref=y_hbm.at[pl.ds(part * share, share), :] if off == 0 else place,
            dst_ref=place,
            send_sem=ys_sem.at[part, off | bit],
            recv_sem=yr_sem.at[part, off | bit],
            device_id=(row, col ^ bit),
            device_id_type=MESH,
        )

    def arrived_y(off, part):
        place = y_v.at[col ^ off, pl.ds(part * share, share), :]
        return pltpu.make_async_remote_copy(
            src_ref=place,
            dst_ref=place,
            send_sem=ys_sem.at[part, off],
            recv_sem=yr_sem.at[part, off],
            device_id=(row, col ^ 1),
            device_id_type=MESH,
        )

    for bit in bits:
        for part in range(parts):
            send_y(0, bit, part).start()

    def pair_of(p, rows):
        return jnp.concatenate([c_v[2 * p, rows, :], c_v[2 * p + 1, rows, :]], axis=1)

    def leads(level):
        return (row >> level) & 1 == 0

    def prepare(level):
        rows, cols = grid_of((width, width))
        vees = jnp.where(cols >= rows, v_v[level], jnp.float32(0.0))
        a_s[level] = stack(vees.T)
        tees = triangle_factor(tt_v[level]).T
        both = jnp.where(leads(level), tees, dot3(stack(vees), tees))
        terms = split(both)
        if level == levels - 1:
            b_s[level, :width], b_s[level, 2 * width : 3 * width] = terms
        else:
            rows, cols = grid_of((width, width))
            after = jnp.where(cols >= rows, v_v[level + 1], jnp.float32(0.0)).T
            folded = split(jnp.where(leads(level + 1), both, dot3(stack(after), both)))
            for i in range(2):
                b_s[level, 2 * i * width : (2 * i + 1) * width] = terms[i]
                b_s[level, (2 * i + 1) * width : (2 * i + 2) * width] = folded[i]

    def take_y(off):
        block = col ^ off
        rows, cols = grid_of((depth, width), block * depth)
        lower = jnp.where(
            rows > cols,
            y_v[block],
            jnp.where(rows == cols, jnp.float32(1.0), jnp.float32(0.0)),
        )
        place = pl.ds(pl.multiple_of(block * depth, depth), depth)
        high, low = split(lower)
        yr_s[0, place, :] = high
        yr_s[1, place, :] = low
        yt_s[off] = stack(lower.T)

    def product(off, p):
        block = col ^ off
        place = pl.ds(pl.multiple_of(block * depth, depth), depth)
        return dot3(yt_s[off], pair_of(p, place))

    load_v.wait()
    load_tt.wait()
    load_t.wait()
    t_s[...] = stack(triangle_factor(t_v[...]).T)
    prepare(0)
    for k in range(chunks):
        load_c(k).wait()
    for p in range(pairs):
        top = pair_of(p, slice(0, width))
        ahead = jnp.where(leads(0), top, dot3(a_s[0], top))
        z_v[0, 2 * p] = ahead[:, :chunk]
        z_v[0, 2 * p + 1] = ahead[:, chunk:]
    own_y.wait()
    take_y(0)
    order = sorted(range(1, n_col), key=lambda off: (bin(off).count("1"), off))
    late = order[1:]

    def arrive(off):
        for part in range(parts):
            arrived_y(off, part).wait_recv()
            for bit in bits:
                if bit < off & -off:
                    send_y(off, bit, part).start()

    for p in range(pairs):
        p_v[p] = product(0, p)
    for off in order[:1]:
        arrive(off)
        take_y(off)
        for p in range(pairs):
            p_v[p] = p_v[p] + product(off, p)
    for level in range(1, levels):
        prepare(level)
    for off in late:
        arrive(off)
        take_y(off)
    upper = jnp.concatenate([yr_s[0, :width, :], yr_s[1, :width, :]], axis=0)
    straight = upper[:width].astype(jnp.float32) + upper[width:].astype(jnp.float32)
    folded = split(jnp.where(leads(0), straight, dot3(a_s[0], straight)))
    for i in range(2):
        f_s[2 * i * width : (2 * i + 1) * width] = yr_s[i, :width, :]
        f_s[(2 * i + 1) * width : (2 * i + 2) * width] = folded[i]

    def exchange(level, k):
        return pltpu.make_async_remote_copy(
            src_ref=z_v.at[level, k],
            dst_ref=r_v.at[level, k],
            send_sem=s_sem.at[level, k],
            recv_sem=r_sem.at[level, k],
            device_id=(row ^ (1 << level), col),
            device_id_type=MESH,
        )

    def local(p):
        proj = p_v[p]
        for off in late:
            proj = proj + product(off, p)
        weight = dot3(t_s[...], proj)
        w_v[p] = weight
        change = dot3(f_s[...], weight)
        for i in range(2):
            k = 2 * p + i
            side = slice(i * chunk, (i + 1) * chunk)
            z_v[0, k] = z_v[0, k] - change[width:, side]
            if i == 0:
                @pl.when(p == 0)
                def _():
                    exchange(0, k).start()
            c_v[k, :width, :] = c_v[k, :width, :] - change[:width, side]

    def combine(level, k):
        top = c_v[k, :width, :]
        ahead = jnp.where(leads(level + 1), top, dot3(a_s[level + 1], top))
        exchange(level, k).wait_recv()
        if level == 0:

            @pl.when(k + 1 < chunks)
            def _():
                exchange(0, k + 1).start()

        change = dot3(b_s[level], z_v[level, k] + r_v[level, k])
        z_v[level + 1, k] = ahead - change[width:]
        exchange(level + 1, k).start()
        c_v[k, :width, :] = top - change[:width]

    def last(k):
        level = levels - 1
        exchange(level, k).wait_recv()
        lhs = jnp.concatenate([b_s[level, :width], b_s[level, 2 * width : 3 * width]], axis=0)
        c_v[k, :width, :] = c_v[k, :width, :] - dot3(lhs, z_v[level, k] + r_v[level, k])

    def store_top(k):
        return pltpu.make_async_copy(
            c_v.at[k, pl.ds(0, width), :], out_hbm.at[pl.ds(0, width), columns(k)], out_sem.at[0, k]
        )

    def store_rest(k):
        return pltpu.make_async_copy(
            c_v.at[k, pl.ds(width, rest), :],
            out_hbm.at[pl.ds(width, rest), columns(k)],
            out_sem.at[1, k],
        )

    local(0)

    def step(t, carry):
        @pl.when((lax.rem(t, 2) == 0) & (t // 2 + 1 < pairs))
        def _():
            local(t // 2 + 1)

        for level in range(levels - 1):
            k = jnp.where(t == 2 * level - 1, 0, t - 2 * level)

            @pl.when((k >= min(level, 1)) & (k < chunks) | (t == 2 * level - 1))
            def _():
                combine(level, k)

        return carry

    lax.fori_loop(0, chunks + 2 * (levels - 2), step, 0)

    def finish(p, carry):
        lhs = jnp.concatenate([yr_s[0, width:, :], yr_s[1, width:, :]], axis=0)
        change = dot3(lhs, w_v[p])
        for i in range(2):
            k = 2 * p + i
            c_v[k, width:, :] = c_v[k, width:, :] - change[:, i * chunk : (i + 1) * chunk]
            store_rest(k).start()
        for i in range(2):
            last(2 * p + i)
            store_top(2 * p + i).start()
        return carry

    lax.fori_loop(0, pairs, finish, 0)

    for bit in bits:
        for off in range(0, n_col, 2 * bit):
            for part in range(parts):
                send_y(off, bit, part).wait_send()

    def drain(k, carry):
        for level in range(levels):
            exchange(level, k).wait_send()
        store_top(k).wait()
        store_rest(k).wait()
        return carry

    lax.fori_loop(0, chunks, drain, 0)


def per_device(trailing, panel_y, panel_t, tree_v, tree_t):
    n_col = lax.axis_size("col")
    depth, width = panel_y.shape
    height, extent = trailing.shape
    levels = tree_v.shape[0]
    chunk = min(CHUNK, extent)
    chunks = extent // chunk
    f32, bf16 = jnp.float32, jnp.bfloat16
    products = height * width * 2 + width * width * (1 + 2 * levels)
    return pl.pallas_call(
        functools.partial(kernel, n_col, levels, chunks, width, depth, PARTS),
        out_shape=pltpu.VMEM(trailing.shape, f32),
        in_specs=[pl.BlockSpec(memory_space=pltpu.HBM)] * 5,
        out_specs=pl.BlockSpec(memory_space=pl.ANY),
        scratch_shapes=[
            pltpu.VMEM((chunks, height, chunk), f32),
            pltpu.VMEM((n_col, depth, width), f32),
            pltpu.VMEM((width, width), f32),
            pltpu.VMEM((levels, width, width), f32),
            pltpu.VMEM((levels, width, width), f32),
            pltpu.VMEM((chunks // 2, width, 2 * chunk), f32),
            pltpu.VMEM((chunks // 2, width, 2 * chunk), f32),
            pltpu.VMEM((levels, chunks, width, chunk), f32),
            pltpu.VMEM((levels, chunks, width, chunk), f32),
            pltpu.VMEM((2, height, width), bf16),
            pltpu.VMEM((n_col, 2 * width, depth), bf16),
            pltpu.VMEM((2 * width, width), bf16),
            pltpu.VMEM((levels, 2 * width, width), bf16),
            pltpu.VMEM((levels, 4 * width, width), bf16),
            pltpu.VMEM((4 * width, width), bf16),
            pltpu.SemaphoreType.DMA((chunks,)),
            pltpu.SemaphoreType.DMA((4,)),
            pltpu.SemaphoreType.DMA((2, chunks)),
            pltpu.SemaphoreType.DMA((PARTS, n_col)),
            pltpu.SemaphoreType.DMA((PARTS, n_col)),
            pltpu.SemaphoreType.DMA((levels, chunks)),
            pltpu.SemaphoreType.DMA((levels, chunks)),
        ],
        compiler_params=pltpu.CompilerParams(
            collective_id=0, has_side_effects=True, vmem_limit_bytes=56 * 1024 * 1024
        ),
        cost_estimate=pl.CostEstimate(
            flops=6 * products * extent,
            bytes_accessed=8 * height * extent,
            transcendentals=0,
        ),
    )(trailing, panel_y, panel_t, tree_v, tree_t)


def solution(mesh):
    placed = (
        P("row", "col"),
        P(("row", "col"), None),
        P("row", None),
        P(None, "row", None),
        P(None, "row", None),
    )
    return jax.shard_map(
        per_device, mesh=mesh, in_specs=placed, out_specs=P("row", "col"), check_vma=False
    )
```
